32 devices in a mesh: rep: 2 (over x), node: 4 (over z), lane: 4 (over y, core).
Axes of the slice: x: 2, y: 2, z: 4, core: 2. Of those that a mesh axis runs over, the one named last changes fastest.
Arguments:
- moe_rows: bfloat16 [64, 7168], P(('rep', 'node', 'lane')), parts along dimension 0, may hold values from -6 to 6
- expert_ids: int32 [64, 8], P(('rep', 'node', 'lane')), parts along dimension 0, may hold values from 0 to 15, all different within a row; in each aligned block of 2 rows (0 to 1, 2 to 3, ...) at most 2 rows name the same one
- route_scores: float32 [64, 8], P(('rep', 'node', 'lane')), parts along dimension 0, may hold values from 0.05 to 1
- gate_proj: bfloat16 [16, 7168, 2048], P('lane', None, 'node'), may hold values from -0.0625 to 0.0625
- up_proj: bfloat16 [16, 7168, 2048], P('lane', None, 'node'), may hold values from -0.0625 to 0.0625
- down_proj: bfloat16 [16, 2048, 7168], P('lane', 'node'), may hold values from -0.125 to 0.125
Outputs:
- moe_out: bfloat16 [64, 7168], P(('rep', 'node', 'lane')), parts along dimension 0
The draws below stay inside these ranges and needn't reach their ends.
There are 2 independent parts, one for each index of `rep`. The reference program is written for one: setup_inputs(seed, part) draws one part's arguments, and reference() takes and returns one part's arrays. A program takes and returns all parts, laid end to end along the dimension named above; an argument that names none is the same for every part. Nothing has to cross between parts.
Inputs may be any that keep to these rules, and one draw needn't show every extreme that they name: `expert_ids`: each row names 8 different experts; the rows of one device name no expert more than 2 times.
All inputs are finite; a program needn't handle non-finite values.
Results may differ from the reference program's by a relative error of at most 0.012.
Values may be sent and summed in bfloat16 or wider, within the bound.
A program may use at most 128 MiB of HBM per device.

```python
import math
import jax
import jax.numpy as jnp
import numpy as np
from jax import lax

D = 7168
TOP = 8
FF_WIN = 2048
EXPERTS = 16
T_DEV = 2
CAP = 2
TOKENS = 32
N_NODE = 4


def steps_of(rng, shape, shards, smallest, high):
    gain, own = 1.0, jax.random.fold_in(rng, 6)
    for axis_at, parts in shards:
        heights = jnp.exp(jax.random.uniform(jax.random.fold_in(own, axis_at), (parts,), jnp.float32, smallest / len(shards), high / len(shards)))
        gain = gain * jnp.repeat(heights, shape[axis_at] // parts).reshape([-1 if axis == axis_at else 1 for axis in range(len(shape))])
    return gain


def deal_out(key, own, number, rows, number_of, top, most, lean):
    order = jax.random.permutation(key, number_of)
    crowded, common = shares(number_of, rows * top, most, lean, True), shares(number_of, rows * top, most, lean, False)
    places = jnp.arange(number_of)

    def named(tallies, offset_by):
        used = int((tallies > 0).sum())
        fixed = max(1, used // 4)
        shifted = fixed + (places - fixed + offset_by * (used - fixed)) % max(1, number_of - fixed)
        return jnp.zeros((number_of,), jnp.int32).at[order[jnp.where(places < fixed, places, shifted)]].set(jnp.asarray(tallies, jnp.int32))

    tallies = jnp.where(number % 4 == 0, named(crowded, number // 4), named(common, number - number // 4 - 1))
    mixed = jax.random.permutation(jax.random.fold_in(own, 3), number_of)
    giver, taker = mixed[0:number_of // 2 * 2:2], mixed[1:number_of // 2 * 2:2]
    slack = jnp.minimum(tallies[giver] - 1, most - tallies[taker]) // 2
    slack = jnp.where((giver == order[0]) | (taker == order[0]) | (tallies[taker] == 0), 0, jnp.maximum(slack, 0))
    shifted = jax.random.randint(jax.random.fold_in(own, 4), (number_of // 2,), 0, 1 << 20) % (slack + 1)
    tallies = tallies.at[giver].add(-shifted).at[taker].add(shifted)
    items = jnp.searchsorted(jnp.cumsum(tallies), jnp.arange(rows * top), side="right").astype(jnp.int32)
    listing = items.reshape(top, rows).T
    listing = listing[jax.random.permutation(jax.random.fold_in(own, 1), rows)]
    offset_by = jax.random.randint(jax.random.fold_in(own, 2), (rows, 1), 0, top)
    return jnp.take_along_axis(listing, (jnp.arange(top)[None, :] + offset_by) % top, axis=1)


def shares(number_of, total, bound, lean, full):
    weights = [(1 << 20) // math.isqrt(grade ** lean) + 1 for grade in range(1, number_of + 1)]
    largest = bound if full else min(bound, max(-(-total // number_of), total * weights[0] // sum(weights)))
    least = 1 if total - largest >= number_of - 1 else 0
    holding, surplus = [largest] + [least] * (number_of - 1), total - largest - least * (number_of - 1)
    while surplus > 0:
        free = [i for i in range(1, number_of) if holding[i] < largest] or [i for i in range(1, number_of) if holding[i] < bound]
        whole, left = sum([weights[i] for i in free]), surplus
        for i in free:
            extra = min(bound - holding[i], max(1, left * weights[i] // whole), surplus)
            holding[i] = holding[i] + extra
            surplus = surplus - extra
    return np.array(holding)


def scatter_about(key, shape, spread, reach, shards=(), kind=jnp.bfloat16):
    entries = spread * jax.random.normal(key, shape, jnp.float32)
    if shards:
        entries = entries * steps_of(key, shape, shards, -0.22, 0.18)
    return jnp.clip(entries, -reach, reach).astype(kind)


def setup_inputs(seed: int = 0, part: int = 0) -> dict:
    key_of = jax.random.split(jax.random.key(seed), 7)
    part_keys = jax.random.split(jax.random.fold_in(key_of[6], part), 7)
    moe_rows = scatter_about(part_keys[0], (TOKENS, D), 1.0, 6.0, ((0, 16),))
    expert_ids_keys = jax.random.split(jax.random.fold_in(part_keys[1], 1), TOKENS // T_DEV)
    expert_ids_turns = jax.random.permutation(jax.random.fold_in(part_keys[1], 3), TOKENS // T_DEV)
    expert_ids = jax.vmap(lambda own, number: deal_out(jax.random.fold_in(part_keys[1], 2), own, number, T_DEV, EXPERTS, TOP, CAP, 2))(expert_ids_keys, expert_ids_turns).reshape((TOKENS, TOP))
    route_scores = jnp.clip(0.05 + 0.95 * jax.random.uniform(part_keys[2], (TOKENS, TOP), jnp.float32) ** steps_of(part_keys[2], (TOKENS, TOP), ((0, 16),), -0.2, 0.2), 0.05, 1.0)
    gate_proj = scatter_about(key_of[3], (EXPERTS, D, FF_WIN), D ** -0.5, 0.0625, ((0, 4), (2, 4)))
    up_proj = scatter_about(key_of[4], (EXPERTS, D, FF_WIN), D ** -0.5, 0.0625, ((0, 4), (2, 4)))
    down_proj = scatter_about(key_of[5], (EXPERTS, FF_WIN, D), FF_WIN ** -0.5, 0.125, ((0, 4), (1, 4)))
    return {"moe_rows": moe_rows, "expert_ids": expert_ids, "route_scores": route_scores, "gate_proj": gate_proj, "up_proj": up_proj, "down_proj": down_proj}


route_factor = 2.5


def reference(moe_rows, expert_ids, route_scores, gate_proj, up_proj, down_proj):
    weights = route_factor * route_scores / jnp.sum(route_scores, axis=1, keepdims=True)
    shard_width = FF_WIN // N_NODE

    def one_expert(running, expert_index):
        gate_val = jnp.dot(moe_rows, gate_proj[expert_index], preferred_element_type=jnp.float32)
        up_val = jnp.dot(moe_rows, up_proj[expert_index], preferred_element_type=jnp.float32)
        hidden = (jax.nn.silu(gate_val) * up_val).astype(jnp.bfloat16)
        down_rows = down_proj[expert_index]
        summed = jnp.zeros((TOKENS, D), jnp.float32)
        for shard_index in range(N_NODE):
            lower = shard_index * shard_width
            term = jnp.dot(hidden[:, lower:lower + shard_width], down_rows[lower:lower + shard_width], preferred_element_type=jnp.float32)
            rounded = lax.optimization_barrier(term.astype(jnp.bfloat16))
            summed = summed + rounded.astype(jnp.float32)
        column = jnp.sum(jnp.where(expert_ids == expert_index, weights, 0.0), axis=1)
        return running + column[:, None] * summed, 0

    start_sum = jnp.zeros((TOKENS, D), jnp.float32)
    total_out, unused = lax.scan(one_expert, start_sum, jnp.arange(EXPERTS, dtype=jnp.int32))
    return total_out.astype(jnp.bfloat16)
```

```python
import functools

import jax
import jax.numpy as jnp
from jax import lax
from jax.experimental import pallas as pl
from jax.experimental.pallas import tpu as pltpu
from jax.sharding import PartitionSpec as P

route_factor = 2.5
MESH = pl.DeviceIdType.MESH
LANES = 128
RING = 16
DOWN_RING = 3


def kernel(
    cfg, rows_ref, ids_ref, scores_ref, gate_hbm, up_hbm, down_hbm, out_ref,
    gate_buf, up_buf, down_buf, pack, mine, gathered, wide, x_buf, w_buf,
    gate_acc, up_acc, hidden, part_buf, send_buf, recv_buf, total,
    gate_sem, up_sem, down_sem, gs_sem, gr_sem, rs_sem, rr_sem,
):
    nodes, lanes, k_step, c_step, stride = cfg
    n = nodes * lanes
    t_dev, width = rows_ref.shape
    experts_here, _, units = gate_hbm.shape
    pieces = width // LANES
    k_steps, c_steps = width // k_step, width // c_step
    steps = experts_here * k_steps
    ring, down_ring = gate_buf.shape[0], down_buf.shape[0]
    per_chunk = c_step // LANES
    block = t_dev * stride
    back = t_dev * per_chunk
    tokens = n * t_dev
    node, lane = lax.axis_index("node"), lax.axis_index("lane")
    me = node * lanes + lane

    def gate_up(step):
        slot = lax.rem(step, ring)
        e, k = step // k_steps, lax.rem(step, k_steps)
        at = pl.ds(pl.multiple_of(k * k_step, k_step), k_step)
        return (
            pltpu.make_async_copy(gate_hbm.at[e, at, :], gate_buf.at[slot], gate_sem.at[slot]),
            pltpu.make_async_copy(up_hbm.at[e, at, :], up_buf.at[slot], up_sem.at[slot]),
        )

    def down(q):
        slot = lax.rem(q, down_ring)
        at = pl.ds(pl.multiple_of(q * c_step, c_step), c_step)
        return pltpu.make_async_copy(down_hbm.at[:, :, at], down_buf.at[slot], down_sem.at[slot])

    def peer(s):
        p = lax.rem(me + s, n)
        return p, {"node": p // lanes, "lane": lax.rem(p, lanes)}

    def start_step(step, _=None):
        for copy in gate_up(step):
            copy.start()
        return 0

    ahead = min(ring, steps)
    lax.fori_loop(0, ahead, start_step, 0)

    barrier = pltpu.get_barrier_semaphore()

    def greet(s, _):
        pl.semaphore_signal(barrier, inc=1, device_id=peer(s)[1], device_id_type=MESH)
        return 0

    lax.fori_loop(1, n, greet, 0)

    ids, scores = ids_ref[...], scores_ref[...]
    weights = route_factor * scores / jnp.sum(scores, axis=1, keepdims=True)
    column = lax.broadcasted_iota(jnp.int32, (t_dev, LANES), 1)
    dense = jnp.zeros((t_dev, LANES), jnp.float32)
    for k in range(ids.shape[1]):
        dense = dense + jnp.where(column == ids[:, k:k + 1], weights[:, k:k + 1], 0.0)
    high = dense.astype(jnp.bfloat16).astype(jnp.float32)
    low = dense - high
    pack[...] = jnp.zeros_like(pack)
    own = rows_ref[...].astype(jnp.float32)
    for i in range(t_dev):
        for c in range(pieces):
            pack[i * stride + c:i * stride + c + 1, :] = own[i:i + 1, c * LANES:(c + 1) * LANES]
        pack[i * stride + pieces:i * stride + pieces + 1, :] = high[i:i + 1, :]
        pack[i * stride + pieces + 1:i * stride + pieces + 2, :] = low[i:i + 1, :]
    packed = pack[...].astype(jnp.bfloat16)
    mine[...] = packed
    gathered[me] = packed

    pl.semaphore_wait(barrier, n - 1)

    def spread(s):
        p, device = peer(s)
        return pltpu.make_async_remote_copy(
            src_ref=mine, dst_ref=gathered.at[me], send_sem=gs_sem.at[s], recv_sem=gr_sem.at[s],
            device_id=device, device_id_type=MESH,
        )

    def spread_start(s, _):
        spread(s).start()
        return 0

    lax.fori_loop(1, n, spread_start, 0)

    def arrive(s, _):
        spread(s).wait_recv()
        return 0

    lax.fori_loop(1, n, arrive, 0)

    def widen(p, _):
        wide[pl.ds(pl.multiple_of(p * block, block), block), :] = gathered[p].astype(jnp.float32)
        return 0

    lax.fori_loop(0, n, widen, 0)
    for c in range(pieces):
        at = c * LANES
        x_buf[at // k_step, :, at % k_step:at % k_step + LANES] = wide[
            pl.ds(c, tokens, stride=stride), :
        ].astype(jnp.bfloat16)
    w_buf[...] = wide[pl.ds(pieces, tokens, stride=stride), :] + wide[pl.ds(pieces + 1, tokens, stride=stride), :]

    def one_expert(e, _):
        gate_acc[...] = jnp.zeros_like(gate_acc)
        up_acc[...] = jnp.zeros_like(up_acc)

        def one_step(k, _):
            step = e * k_steps + k
            slot = lax.rem(step, ring)
            for copy in gate_up(step):
                copy.wait()
            x = x_buf[k]
            gate_acc[...] += jnp.dot(x, gate_buf[slot], preferred_element_type=jnp.float32)
            up_acc[...] += jnp.dot(x, up_buf[slot], preferred_element_type=jnp.float32)

            @pl.when(step + ring < steps)
            def _():
                start_step(step + ring)

            for q in range(min(down_ring, c_steps)):
                @pl.when(step == max(steps - ring, 0) + q)
                def _():
                    down(q).start()

            return 0

        lax.fori_loop(0, k_steps, one_step, 0)
        pick = lax.broadcasted_iota(jnp.int32, w_buf.shape, 1) == lane * experts_here + e
        weight = jnp.sum(jnp.where(pick, w_buf[...], 0.0), axis=1, keepdims=True)
        g = gate_acc[...]
        hidden[e] = (weight * (g / (1.0 + jnp.exp(-g)) * up_acc[...])).astype(jnp.bfloat16)
        return 0

    lax.fori_loop(0, experts_here, one_expert, 0)

    def give(q, s):
        p, device = peer(s)
        return pltpu.make_async_remote_copy(
            src_ref=send_buf.at[q, p], dst_ref=recv_buf.at[q, me],
            send_sem=rs_sem.at[q, s], recv_sem=rr_sem.at[q, s],
            device_id=device, device_id_type=MESH,
        )

    def one_chunk(q, _):
        slot = lax.rem(q, down_ring)
        down(q).wait()
        part = jnp.dot(hidden[0], down_buf[slot, 0], preferred_element_type=jnp.float32)
        for e in range(1, experts_here):
            part = part + jnp.dot(hidden[e], down_buf[slot, e], preferred_element_type=jnp.float32)
        for c in range(per_chunk):
            part_buf[pl.ds(c, tokens, stride=per_chunk), :] = part[:, c * LANES:(c + 1) * LANES]
        send_buf[q] = part_buf[...].astype(jnp.bfloat16).reshape((n, back, LANES))

        @pl.when(q + down_ring < c_steps)
        def _():
            down(q + down_ring).start()

        def give_start(s, _):
            give(q, s).start()
            return 0

        lax.fori_loop(1, n, give_start, 0)
        return 0

    lax.fori_loop(0, c_steps, one_chunk, 0)

    def sum_chunk(q, _):
        def taken(s, _):
            give(q, s).wait_recv()
            return 0

        lax.fori_loop(1, n, taken, 0)
        recv_buf[q, me] = send_buf[q, me]
        total[pl.ds(pl.multiple_of(q * back, back), back), :] = jnp.sum(
            recv_buf[q].astype(jnp.float32), axis=0
        )
        return 0

    lax.fori_loop(0, c_steps, sum_chunk, 0)
    for q in range(c_steps):
        for c in range(per_chunk):
            at = q * c_step + c * LANES
            out_ref[:, at:at + LANES] = total[pl.ds(q * back + c, t_dev, stride=per_chunk), :].astype(out_ref.dtype)

    def left(s, _):
        spread(s).wait_send()

        def each(q, _):
            give(q, s).wait_send()
            return 0

        lax.fori_loop(0, c_steps, each, 0)
        return 0

    lax.fori_loop(1, n, left, 0)


def on_device(moe_rows, expert_ids, route_scores, gate_proj, up_proj, down_proj):
    nodes, lanes = lax.axis_size("node"), lax.axis_size("lane")
    n = nodes * lanes
    t_dev, width = moe_rows.shape
    experts_here, _, units = gate_proj.shape
    k_step = c_step = 1024
    stride = -(-(width // LANES + 2) // 16) * 16
    tokens = n * t_dev
    per_chunk = c_step // LANES
    ring = min(RING, experts_here * (width // k_step))
    down_ring = min(DOWN_RING, width // c_step)
    bf16, f32 = jnp.bfloat16, jnp.float32
    vmem, hbm = pl.BlockSpec(memory_space=pltpu.VMEM), pl.BlockSpec(memory_space=pl.ANY)
    return pl.pallas_call(
        functools.partial(kernel, (nodes, lanes, k_step, c_step, stride)),
        out_shape=jax.ShapeDtypeStruct((t_dev, width), bf16),
        in_specs=[vmem, vmem, vmem, hbm, hbm, hbm],
        out_specs=vmem,
        scratch_shapes=[
            pltpu.VMEM((ring, k_step, units), bf16),
            pltpu.VMEM((ring, k_step, units), bf16),
            pltpu.VMEM((down_ring, experts_here, units, c_step), bf16),
            pltpu.VMEM((t_dev * stride, LANES), f32),
            pltpu.VMEM((t_dev * stride, LANES), bf16),
            pltpu.VMEM((n, t_dev * stride, LANES), bf16),
            pltpu.VMEM((tokens * stride, LANES), f32),
            pltpu.VMEM((width // k_step, tokens, k_step), bf16),
            pltpu.VMEM((tokens, LANES), f32),
            pltpu.VMEM((tokens, units), f32),
            pltpu.VMEM((tokens, units), f32),
            pltpu.VMEM((experts_here, tokens, units), bf16),
            pltpu.VMEM((tokens * per_chunk, LANES), f32),
            pltpu.VMEM((width // c_step, n, t_dev * per_chunk, LANES), bf16),
            pltpu.VMEM((width // c_step, n, t_dev * per_chunk, LANES), bf16),
            pltpu.VMEM((t_dev * width // LANES, LANES), f32),
            pltpu.SemaphoreType.DMA((ring,)),
            pltpu.SemaphoreType.DMA((ring,)),
            pltpu.SemaphoreType.DMA((down_ring,)),
            pltpu.SemaphoreType.DMA((n,)),
            pltpu.SemaphoreType.DMA((n,)),
            pltpu.SemaphoreType.DMA((width // c_step, n)),
            pltpu.SemaphoreType.DMA((width // c_step, n)),
        ],
        compiler_params=pltpu.CompilerParams(
            collective_id=0, has_side_effects=True, vmem_limit_bytes=60 * 2**20
        ),
        cost_estimate=pl.CostEstimate(
            flops=6 * tokens * experts_here * width * units,
            bytes_accessed=6 * experts_here * width * units,
            transcendentals=tokens * experts_here * units,
        ),
    )(moe_rows, expert_ids, route_scores, gate_proj, up_proj, down_proj)


def solution(mesh):
    in_specs = (
        P(("rep", "node", "lane"), None),
        P(("rep", "node", "lane"), None),
        P(("rep", "node", "lane"), None),
        P("lane", None, "node"),
        P("lane", None, "node"),
        P("lane", "node", None),
    )
    out_specs = P(("rep", "node", "lane"), None)
    return jax.shard_map(
        on_device, mesh=mesh, in_specs=in_specs, out_specs=out_specs, check_vma=False
    )
```

```python
import functools

import jax
import jax.numpy as jnp
from jax import lax
from jax.experimental import pallas as pl
from jax.experimental.pallas import tpu as pltpu
from jax.sharding import PartitionSpec as P

route_factor = 2.5
MESH = pl.DeviceIdType.MESH
LANES = 128
RING = 20
DOWN_RING = 3
LAG = 3
FIRST = 5


def kernel(
    cfg, rows_ref, ids_ref, scores_ref, gate_hbm, up_hbm, down_hbm, out_ref,
    gate_buf, up_buf, down_buf, pack, gathered, wide, x_buf, w_buf,
    gate_acc, up_acc, hidden, part_buf, lane_out, lane_in, node_out, node_in, total,
    gate_sem, up_sem, down_sem, zs_sem, zr_sem, fs_sem, fr_sem, ls_sem, lr_sem, ns_sem, nr_sem,
):
    nodes, lanes, k_step, c_step, stride = cfg
    n = nodes * lanes
    t_dev, width = rows_ref.shape
    experts_here, _, units = gate_hbm.shape
    pieces = width // LANES
    k_steps, c_steps = width // k_step, width // c_step
    steps = experts_here * k_steps
    ring, down_ring = gate_buf.shape[0], down_buf.shape[0]
    per_chunk = c_step // LANES
    block = t_dev * stride
    back = t_dev * per_chunk
    tokens = n * t_dev
    node, lane = lax.axis_index("node"), lax.axis_index("lane")

    def gate_up(step):
        slot = lax.rem(step, ring)
        e, k = step // k_steps, lax.rem(step, k_steps)
        at = pl.ds(pl.multiple_of(k * k_step, k_step), k_step)
        return (
            pltpu.make_async_copy(gate_hbm.at[e, at, :], gate_buf.at[slot], gate_sem.at[slot]),
            pltpu.make_async_copy(up_hbm.at[e, at, :], up_buf.at[slot], up_sem.at[slot]),
        )

    def down(q):
        slot = lax.rem(q, down_ring)
        at = pl.ds(pl.multiple_of(q * c_step, c_step), c_step)
        return pltpu.make_async_copy(down_hbm.at[:, :, at], down_buf.at[slot], down_sem.at[slot])

    def node_at(s):
        return lax.rem(node + s, nodes)

    def lane_at(s):
        return lax.rem(lane + s, lanes)

    def start_step(step, _=None):
        for copy in gate_up(step):
            copy.start()
        return 0

    barrier = pltpu.get_barrier_semaphore()

    for s in range(1, nodes):
        pl.semaphore_signal(barrier, inc=1, device_id={"node": node_at(s)}, device_id_type=MESH)
    for s in range(1, lanes):
        pl.semaphore_signal(barrier, inc=1, device_id={"lane": lane_at(s)}, device_id_type=MESH)

    ahead = min(ring, steps)
    first = min(FIRST, ahead)
    lax.fori_loop(0, first, start_step, 0)

    ids, scores = ids_ref[...], scores_ref[...]
    weights = route_factor * scores / jnp.sum(scores, axis=1, keepdims=True)
    column = lax.broadcasted_iota(jnp.int32, (t_dev, LANES), 1)
    dense = jnp.zeros((t_dev, LANES), jnp.float32)
    for k in range(ids.shape[1]):
        dense = dense + jnp.where(column == ids[:, k:k + 1], weights[:, k:k + 1], 0.0)
    high = dense.astype(jnp.bfloat16).astype(jnp.float32)
    low = dense - high
    pack[...] = jnp.zeros_like(pack)
    own = rows_ref[...].astype(jnp.float32)
    for i in range(t_dev):
        for c in range(pieces):
            pack[i * stride + c:i * stride + c + 1, :] = own[i:i + 1, c * LANES:(c + 1) * LANES]
        pack[i * stride + pieces:i * stride + pieces + 1, :] = high[i:i + 1, :]
        pack[i * stride + pieces + 1:i * stride + pieces + 2, :] = low[i:i + 1, :]
    gathered[lane * nodes + node] = pack[...].astype(jnp.bfloat16)

    pl.semaphore_wait(barrier, nodes + lanes - 2)

    def across(s):
        return pltpu.make_async_remote_copy(
            src_ref=gathered.at[lane * nodes + node], dst_ref=gathered.at[lane * nodes + node],
            send_sem=zs_sem.at[s], recv_sem=zr_sem.at[s],
            device_id={"node": node_at(s)}, device_id_type=MESH,
        )

    def forward(s, t):
        at = lane * nodes + node_at(nodes - s)
        return pltpu.make_async_remote_copy(
            src_ref=gathered.at[at], dst_ref=gathered.at[at],
            send_sem=fs_sem.at[s, t], recv_sem=fr_sem.at[s, t],
            device_id={"lane": lane_at(t)}, device_id_type=MESH,
        )

    for s in range(1, nodes):
        across(s).start()
    for t in range(1, lanes):
        forward(0, t).start()
    lax.fori_loop(first, ahead, start_step, 0)
    for q in range(down_ring):
        down(q).start()
    for s in range(1, nodes):
        across(s).wait_recv()
        for t in range(1, lanes):
            forward(s, t).start()
    for s in range(nodes):
        for t in range(1, lanes):
            forward(s, t).wait_recv()

    def widen(p, _):
        wide[pl.ds(pl.multiple_of(p * block, block), block), :] = gathered[p].astype(jnp.float32)
        return 0

    lax.fori_loop(0, n, widen, 0)
    for c in range(pieces):
        at = c * LANES
        x_buf[at // k_step, :, at % k_step:at % k_step + LANES] = wide[
            pl.ds(c, tokens, stride=stride), :
        ].astype(jnp.bfloat16)
    w_buf[...] = wide[pl.ds(pieces, tokens, stride=stride), :] + wide[pl.ds(pieces + 1, tokens, stride=stride), :]

    def one_expert(e, _):
        gate_acc[...] = jnp.zeros_like(gate_acc)
        up_acc[...] = jnp.zeros_like(up_acc)

        def one_step(k, _):
            step = e * k_steps + k
            slot = lax.rem(step, ring)
            for copy in gate_up(step):
                copy.wait()
            x = x_buf[k]
            gate_acc[...] += jnp.dot(x, gate_buf[slot], preferred_element_type=jnp.float32)
            up_acc[...] += jnp.dot(x, up_buf[slot], preferred_element_type=jnp.float32)

            @pl.when(step + ring < steps)
            def _():
                start_step(step + ring)

            return 0

        lax.fori_loop(0, k_steps, one_step, 0)
        pick = lax.broadcasted_iota(jnp.int32, w_buf.shape, 1) == lane * experts_here + e
        weight = jnp.sum(jnp.where(pick, w_buf[...], 0.0), axis=1, keepdims=True)
        g = gate_acc[...]
        hidden[e] = (weight * (g / (1.0 + jnp.exp(-g)) * up_acc[...])).astype(jnp.bfloat16)
        return 0

    lax.fori_loop(0, experts_here, one_expert, 0)

    def to_lane(q, s):
        return pltpu.make_async_remote_copy(
            src_ref=lane_out.at[q, lane_at(s)], dst_ref=lane_in.at[q, lane],
            send_sem=ls_sem.at[q, s], recv_sem=lr_sem.at[q, s],
            device_id={"lane": lane_at(s)}, device_id_type=MESH,
        )

    def to_node(q, s):
        return pltpu.make_async_remote_copy(
            src_ref=node_out.at[q, node_at(s)], dst_ref=node_in.at[q, node],
            send_sem=ns_sem.at[q, s], recv_sem=nr_sem.at[q, s],
            device_id={"node": node_at(s)}, device_id_type=MESH,
        )

    def lane_sum(q):
        for s in range(1, lanes):
            to_lane(q, s).wait_recv()
        lane_in[q, lane] = lane_out[q, lane]
        summed = jnp.sum(lane_in[q].astype(jnp.float32), axis=0)
        node_out[q] = summed.astype(jnp.bfloat16).reshape((nodes, back, LANES))
        for s in range(1, nodes):
            to_node(q, s).start()

    def one_chunk(q, _):
        slot = lax.rem(q, down_ring)
        down(q).wait()
        part = jnp.dot(hidden[0], down_buf[slot, 0], preferred_element_type=jnp.float32)
        for e in range(1, experts_here):
            part = part + jnp.dot(hidden[e], down_buf[slot, e], preferred_element_type=jnp.float32)
        for c in range(per_chunk):
            part_buf[pl.ds(c, tokens, stride=per_chunk), :] = part[:, c * LANES:(c + 1) * LANES]
        lane_out[q] = part_buf[...].astype(jnp.bfloat16).reshape((lanes, nodes * back, LANES))
        for s in range(1, lanes):
            to_lane(q, s).start()

        @pl.when(q + down_ring < c_steps)
        def _():
            down(q + down_ring).start()

        @pl.when(q >= LAG)
        def _():
            lane_sum(q - LAG)

        return 0

    lax.fori_loop(0, c_steps, one_chunk, 0)

    def late(q, _):
        lane_sum(q)
        return 0

    lax.fori_loop(max(c_steps - LAG, 0), c_steps, late, 0)

    def sum_chunk(q, _):
        for s in range(1, nodes):
            to_node(q, s).wait_recv()
        node_in[q, node] = node_out[q, node]
        total[pl.ds(pl.multiple_of(q * back, back), back), :] = jnp.sum(
            node_in[q].astype(jnp.float32), axis=0
        )
        return 0

    lax.fori_loop(0, c_steps, sum_chunk, 0)
    for q in range(c_steps):
        for c in range(per_chunk):
            at = q * c_step + c * LANES
            out_ref[:, at:at + LANES] = total[pl.ds(q * back + c, t_dev, stride=per_chunk), :].astype(out_ref.dtype)

    for s in range(1, nodes):
        across(s).wait_send()
    for s in range(nodes):
        for t in range(1, lanes):
            forward(s, t).wait_send()

    def left(q, _):
        for s in range(1, lanes):
            to_lane(q, s).wait_send()
        for s in range(1, nodes):
            to_node(q, s).wait_send()
        return 0

    lax.fori_loop(0, c_steps, left, 0)


def on_device(moe_rows, expert_ids, route_scores, gate_proj, up_proj, down_proj):
    nodes, lanes = lax.axis_size("node"), lax.axis_size("lane")
    n = nodes * lanes
    t_dev, width = moe_rows.shape
    experts_here, _, units = gate_proj.shape
    k_step = c_step = 1024
    stride = -(-(width // LANES + 2) // 16) * 16
    tokens = n * t_dev
    per_chunk = c_step // LANES
    ring = min(RING, experts_here * (width // k_step))
    down_ring = min(DOWN_RING, width // c_step)
    bf16, f32 = jnp.bfloat16, jnp.float32
    vmem, hbm = pl.BlockSpec(memory_space=pltpu.VMEM), pl.BlockSpec(memory_space=pl.ANY)
    return pl.pallas_call(
        functools.partial(kernel, (nodes, lanes, k_step, c_step, stride)),
        out_shape=jax.ShapeDtypeStruct((t_dev, width), bf16),
        in_specs=[vmem, vmem, vmem, hbm, hbm, hbm],
        out_specs=vmem,
        scratch_shapes=[
            pltpu.VMEM((ring, k_step, units), bf16),
            pltpu.VMEM((ring, k_step, units), bf16),
            pltpu.VMEM((down_ring, experts_here, units, c_step), bf16),
            pltpu.VMEM((t_dev * stride, LANES), f32),
            pltpu.VMEM((n, t_dev * stride, LANES), bf16),
            pltpu.VMEM((tokens * stride, LANES), f32),
            pltpu.VMEM((width // k_step, tokens, k_step), bf16),
            pltpu.VMEM((tokens, LANES), f32),
            pltpu.VMEM((tokens, units), f32),
            pltpu.VMEM((tokens, units), f32),
            pltpu.VMEM((experts_here, tokens, units), bf16),
            pltpu.VMEM((tokens * per_chunk, LANES), f32),
            pltpu.VMEM((width // c_step, lanes, nodes * t_dev * per_chunk, LANES), bf16),
            pltpu.VMEM((width // c_step, lanes, nodes * t_dev * per_chunk, LANES), bf16),
            pltpu.VMEM((width // c_step, nodes, t_dev * per_chunk, LANES), bf16),
            pltpu.VMEM((width // c_step, nodes, t_dev * per_chunk, LANES), bf16),
            pltpu.VMEM((t_dev * width // LANES, LANES), f32),
            pltpu.SemaphoreType.DMA((ring,)),
            pltpu.SemaphoreType.DMA((ring,)),
            pltpu.SemaphoreType.DMA((down_ring,)),
            pltpu.SemaphoreType.DMA((nodes,)),
            pltpu.SemaphoreType.DMA((nodes,)),
            pltpu.SemaphoreType.DMA((nodes, lanes)),
            pltpu.SemaphoreType.DMA((nodes, lanes)),
            pltpu.SemaphoreType.DMA((width // c_step, lanes)),
            pltpu.SemaphoreType.DMA((width // c_step, lanes)),
            pltpu.SemaphoreType.DMA((width // c_step, nodes)),
            pltpu.SemaphoreType.DMA((width // c_step, nodes)),
        ],
        compiler_params=pltpu.CompilerParams(
            collective_id=0, has_side_effects=True, vmem_limit_bytes=60 * 2**20
        ),
        cost_estimate=pl.CostEstimate(
            flops=6 * tokens * experts_here * width * units,
            bytes_accessed=6 * experts_here * width * units,
            transcendentals=tokens * experts_here * units,
        ),
    )(moe_rows, expert_ids, route_scores, gate_proj, up_proj, down_proj)


def solution(mesh):
    in_specs = (
        P(("rep", "node", "lane"), None),
        P(("rep", "node", "lane"), None),
        P(("rep", "node", "lane"), None),
        P("lane", None, "node"),
        P("lane", None, "node"),
        P("lane", "node", None),
    )
    out_specs = P(("rep", "node", "lane"), None)
    return jax.shard_map(
        on_device, mesh=mesh, in_specs=in_specs, out_specs=out_specs, check_vma=False
    )
```
